128 devices in a mesh: pipe: 8 (over x_hi, z), expert: 16 (over y, x_lo, core).
Axes of the slice: x: 4 (x_hi: 2, x_lo: 2; x = x_hi * 2 + x_lo), y: 4, z: 4, core: 2. Of those that a mesh axis runs over, the one named last changes fastest.
Arguments:
- onward_block_activation: bfloat16 [8, 2048, 4096], P('pipe', 'expert'), may hold values from -40 to 40
- reverse_stored_activation: bfloat16 [8, 2048, 4096], P('pipe', 'expert'), may hold values from -40 to 40
- reverse_result_derivative: bfloat16 [8, 2048, 4096], P('pipe', 'expert'), may hold values from -6 to 6
- onward_specialist_choices: int32 [8, 2048, 2], P('pipe', 'expert'), may hold values from 0 to 15, as said below
- reverse_specialist_choices: int32 [8, 2048, 2], P('pipe', 'expert'), may hold values from 0 to 15, as said below
- onward_mixing_coefficients: float32 [8, 2048, 2], P('pipe', 'expert'), may hold values from 0.1 to 1
- reverse_mixing_coefficients: float32 [8, 2048, 2], P('pipe', 'expert'), may hold values from 0.1 to 1
- quota_table: int32 [8, 16], P('pipe'), may hold values from 16 to 32, as said below
- rescaling_factor_list: float32 [8, 4096], P('pipe'), may hold values from 0.1 to 1.9
- gating_projection_matrix: bfloat16 [8, 16, 4096, 768], P('pipe', 'expert'), may hold values from -0.09375 to 0.09375
- expansion_matrix: bfloat16 [8, 16, 4096, 768], P('pipe', 'expert'), may hold values from -0.09375 to 0.09375
- contraction_matrix: bfloat16 [8, 16, 768, 4096], P('pipe', 'expert'), may hold values from -0.21875 to 0.21875
Outputs:
- fwd_next: bfloat16 [8, 2048, 4096], P('pipe', 'expert')
- grad_next: bfloat16 [8, 2048, 4096], P('pipe', 'expert')
The draws below stay inside these ranges and needn't reach their ends.
Inputs may be any that keep to these rules, and one draw needn't show every extreme that they name: `onward_specialist_choices`: each row names two different experts. In every section one expert has capacity 32 and is named by 32 or more entries of every aligned block of 128 tokens, in both micro-batches. `reverse_specialist_choices`: each row names two different experts, with the same property as onward_specialist_choices. `quota_table`: in every section one expert has capacity 32.
All inputs are finite; a program needn't handle non-finite values.
Results may differ from the reference program's by a relative error of at most 0.0053.
Values may be sent and summed in bfloat16 or wider, within the bound.
No kernel may reach another device: no remote copies, remote signals or barrier semaphores. Data moves between devices by JAX's collectives and lax.ppermute only.
A program may use at most 128 MiB of HBM per device.

```python
import jax
import jax.numpy as jnp
from jax import lax

D = 4096
HID = 768
TOP_K = 2
TOK_DEV = 128
CAP = 32
EXPERTS = 16
SECTIONS = 8
TOKENS = 2048


def busiest_experts(key):
    return jax.random.randint(jax.random.fold_in(key, 7), (SECTIONS,), 0, EXPERTS)


def shuffle_block(subkey):
    return jax.random.permutation(subkey, TOK_DEV)


def make_routes(key, salt_value):
    busiest = busiest_experts(key)
    route_key = jax.random.fold_in(key, salt_value)
    blocks = TOKENS // TOK_DEV
    perm_keys = jax.random.split(jax.random.fold_in(route_key, 1), SECTIONS * blocks)
    placing = jax.vmap(shuffle_block)(perm_keys).reshape(SECTIONS, TOKENS)
    first_other = jax.random.randint(jax.random.fold_in(route_key, 2), (SECTIONS, TOKENS), 0, EXPERTS - 1)
    second_step = jax.random.randint(jax.random.fold_in(route_key, 3), (SECTIONS, TOKENS), 0, EXPERTS - 1)
    busy_col = busiest[:, None]
    first_pick = jnp.where(placing < CAP, busy_col, (busy_col + 1 + first_other) % EXPERTS)
    second_pick = (first_pick + 1 + second_step) % EXPERTS
    return jnp.stack([first_pick, second_pick], axis=-1).astype(jnp.int32)


def draw_onward_specialist_choices(key, part):
    return make_routes(key, 11)


def draw_reverse_specialist_choices(key, part):
    return make_routes(key, 13)


def draw_quota_table(key, part):
    busiest = busiest_experts(key)
    drawn = jax.random.randint(jax.random.fold_in(key, 17), (SECTIONS, EXPERTS), CAP // 2, CAP + 1)
    chosen = jnp.arange(EXPERTS, dtype=jnp.int32)[None, :] == busiest[:, None]
    return jnp.where(chosen, CAP, drawn).astype(jnp.int32)


def spread_rows(key):
    row_scale = jnp.exp(jax.random.uniform(jax.random.fold_in(key, 1), (SECTIONS, TOKENS, 1), jnp.float32, -1.15, 1.15))
    col_scale = jnp.exp(jax.random.uniform(jax.random.fold_in(key, 2), (SECTIONS, 1, D), jnp.float32, -1.15, 1.15))
    values = jax.random.normal(jax.random.fold_in(key, 3), (SECTIONS, TOKENS, D), jnp.float32)
    values = jnp.clip(values, -4.0, 4.0)
    return (values * row_scale * col_scale).astype(jnp.bfloat16)


def draw_onward_block_activation(key, part):
    return spread_rows(jax.random.fold_in(key, 21))


def draw_reverse_stored_activation(key, part):
    return spread_rows(jax.random.fold_in(key, 23))


def shard_levels(own_key, extent, pieces, low, top_value):
    factor_of = 1.0
    for axis_at, parts in pieces:
        draws = jax.random.uniform(jax.random.fold_in(jax.random.fold_in(own_key, 6), axis_at), (parts,), jnp.float32, low / len(pieces), top_value / len(pieces))
        factor_of = factor_of * jnp.repeat(jnp.exp(draws), extent[axis_at] // parts).reshape((-1,) + (1,) * (len(extent) - 1 - axis_at))
    return factor_of


def scatter_about(key, dims, deviation, most, pieces=(), held_as=jnp.bfloat16):
    array = deviation * jax.random.normal(key, dims, jnp.float32)
    if pieces:
        array = array * shard_levels(key, dims, pieces, -0.22, 0.18)
    return jnp.clip(array, -most, most).astype(held_as)


def setup_inputs(seed: int = 0) -> dict:
    streams_of = jax.random.split(jax.random.key(seed), 13)
    onward_block_activation = draw_onward_block_activation(jax.random.fold_in(streams_of[12], 71), 0)
    reverse_stored_activation = draw_reverse_stored_activation(jax.random.fold_in(streams_of[12], 71), 0)
    reverse_result_derivative = scatter_about(streams_of[2], (SECTIONS, TOKENS, D), 1.0, 6.0, ((0, 8), (1, 16)))
    onward_specialist_choices = draw_onward_specialist_choices(jax.random.fold_in(streams_of[12], 71), 0)
    reverse_specialist_choices = draw_reverse_specialist_choices(jax.random.fold_in(streams_of[12], 71), 0)
    onward_mixing_coefficients = jnp.clip(0.1 + 0.9 * jax.random.uniform(streams_of[5], (SECTIONS, TOKENS, TOP_K), jnp.float32) ** shard_levels(streams_of[5], (SECTIONS, TOKENS, TOP_K), ((0, 8), (1, 16)), -0.2, 0.2), 0.1, 1.0)
    reverse_mixing_coefficients = jnp.clip(0.1 + 0.9 * jax.random.uniform(streams_of[6], (SECTIONS, TOKENS, TOP_K), jnp.float32) ** shard_levels(streams_of[6], (SECTIONS, TOKENS, TOP_K), ((0, 8), (1, 16)), -0.2, 0.2), 0.1, 1.0)
    quota_table = draw_quota_table(jax.random.fold_in(streams_of[12], 71), 0)
    rescaling_factor_list = jnp.clip(1.0 + 0.18 * jax.random.normal(streams_of[8], (SECTIONS, D), jnp.float32), 0.1, 1.9)
    gating_projection_matrix = scatter_about(streams_of[9], (SECTIONS, EXPERTS, D, HID), D ** -0.5, 0.09375, ((0, 8), (1, 16)))
    expansion_matrix = scatter_about(streams_of[10], (SECTIONS, EXPERTS, D, HID), D ** -0.5, 0.09375, ((0, 8), (1, 16)))
    contraction_matrix = scatter_about(streams_of[11], (SECTIONS, EXPERTS, HID, D), HID ** -0.5, 0.21875, ((0, 8), (1, 16)))
    return {"onward_block_activation": onward_block_activation, "reverse_stored_activation": reverse_stored_activation, "reverse_result_derivative": reverse_result_derivative, "onward_specialist_choices": onward_specialist_choices, "reverse_specialist_choices": reverse_specialist_choices, "onward_mixing_coefficients": onward_mixing_coefficients, "reverse_mixing_coefficients": reverse_mixing_coefficients, "quota_table": quota_table, "rescaling_factor_list": rescaling_factor_list, "gating_projection_matrix": gating_projection_matrix, "expansion_matrix": expansion_matrix, "contraction_matrix": contraction_matrix}


EPSILON = 1e-06

def normalize(rows_in, scaling):
    values = rows_in.astype(jnp.float32)
    inverse = lax.rsqrt(lax.optimization_barrier(jnp.mean(values * values, axis=-1, keepdims=True)) + EPSILON)
    return (values, inverse, (values * inverse * scaling).astype(jnp.bfloat16))

def block_plan(routes, specialist_quota_bounds):
    top = routes.shape[1]
    count = specialist_quota_bounds.shape[0]
    flat_ids = routes.reshape(-1)
    onehot = (flat_ids[:, None] == jnp.arange(count, dtype=jnp.int32)[None, :]).astype(jnp.int32)
    before = jnp.cumsum(onehot, axis=0) - onehot
    rank_in = lax.optimization_barrier(jnp.sum(before * onehot, axis=1))
    limits = lax.optimization_barrier(jnp.sum(onehot * specialist_quota_bounds[None, :], axis=1))
    kept_mask = (rank_in < limits).astype(jnp.int32)
    slot_of = jnp.where(kept_mask > 0, flat_ids * CAP + rank_in, count * CAP).astype(jnp.int32)
    entries = jnp.arange(flat_ids.shape[0], dtype=jnp.int32)
    slot_entry = jnp.zeros((count * CAP + 1,), jnp.int32).at[slot_of].set(entries)[:-1]
    filled = jnp.zeros((count * CAP + 1,), jnp.int32).at[slot_of].set(1)[:-1]
    return (slot_of.reshape(routes.shape), kept_mask.reshape(routes.shape), slot_entry, filled)

def expert_forward(rows, gate_w, up_w, down_w):
    gate_pre = jnp.dot(rows, gate_w, preferred_element_type=jnp.float32)
    up_pre = jnp.dot(rows, up_w, preferred_element_type=jnp.float32)
    hidden = (jax.nn.silu(gate_pre) * up_pre).astype(jnp.bfloat16)
    return jnp.dot(hidden, down_w, preferred_element_type=jnp.float32).astype(jnp.bfloat16)

def expert_backward(rows, grads, gate_w, up_w, down_w):
    contract = (((1,), (1,)), ((), ()))
    gate_pre = jnp.dot(rows, gate_w, preferred_element_type=jnp.float32)
    up_pre = jnp.dot(rows, up_w, preferred_element_type=jnp.float32)
    hidden_grad = lax.dot_general(grads, down_w, contract, preferred_element_type=jnp.float32)
    sigmoid_gate = jax.nn.sigmoid(gate_pre)
    gate_grad = (hidden_grad * up_pre * sigmoid_gate * (1.0 + gate_pre * (1.0 - sigmoid_gate))).astype(jnp.bfloat16)
    up_grad = (hidden_grad * gate_pre * sigmoid_gate).astype(jnp.bfloat16)
    summed = lax.dot_general(gate_grad, gate_w, contract, preferred_element_type=jnp.float32)
    summed = summed + lax.dot_general(up_grad, up_w, contract, preferred_element_type=jnp.float32)
    return summed.astype(jnp.bfloat16)

def pick_rows(table, index):
    return table[index]

def run_forward_expert(items):
    return expert_forward(items[0], items[1], items[2], items[3])

def run_backward_expert(items):
    return expert_backward(items[0], items[1], items[2], items[3], items[4])

def segment_clock_sweep(fwd_x, saved_x, grad_y, routes_f, routes_b, weights_f, weights_b, specialist_quota_bounds, scaling, gate_w, up_w, down_w):
    blocks = TOKENS // TOK_DEV
    slots = EXPERTS * CAP
    zero_bf = jnp.zeros((), jnp.bfloat16)
    values_f, inverse_f, normed_f = normalize(fwd_x, scaling)
    values_b, inverse_b, normed_b = normalize(saved_x, scaling)
    plan_f = jax.vmap(block_plan, in_axes=(0, None))(routes_f.reshape(blocks, TOK_DEV, TOP_K), specialist_quota_bounds)
    plan_b = jax.vmap(block_plan, in_axes=(0, None))(routes_b.reshape(blocks, TOK_DEV, TOP_K), specialist_quota_bounds)
    offsets = (jnp.arange(blocks, dtype=jnp.int32) * TOK_DEV)[:, None]
    token_f = plan_f[2] // TOP_K + offsets
    token_b = plan_b[2] // TOP_K + offsets
    mask_f = plan_f[3][..., None] > 0
    mask_b = plan_b[3][..., None] > 0
    rows_f = jnp.where(mask_f, normed_f[token_f], zero_bf)
    rows_b = jnp.where(mask_b, normed_b[token_b], zero_bf)
    scale_b = jnp.take_along_axis(weights_b.reshape(blocks, TOK_DEV * TOP_K), plan_b[2], axis=1)
    grads_b = jnp.where(mask_b, (scale_b[..., None] * grad_y[token_b].astype(jnp.float32)).astype(jnp.bfloat16), zero_bf)

    def by_expert(blocked):
        return blocked.reshape(blocks, EXPERTS, CAP, D).transpose(1, 0, 2, 3).reshape(EXPERTS, blocks * CAP, D)

    def to_blocks(grouped):
        return grouped.reshape(EXPERTS, blocks, CAP, D).transpose(1, 0, 2, 3).reshape(blocks, slots, D)
    out_f = to_blocks(lax.map(run_forward_expert, (by_expert(rows_f), gate_w, up_w, down_w)))
    out_b = to_blocks(lax.map(run_backward_expert, (by_expert(rows_b), by_expert(grads_b), gate_w, up_w, down_w)))
    picked_f = jax.vmap(pick_rows)(out_f, jnp.minimum(plan_f[0], slots - 1))
    coeff_f = weights_f.reshape(blocks, TOK_DEV, TOP_K) * plan_f[1]
    summed_f = lax.optimization_barrier(jnp.sum(coeff_f[..., None] * picked_f.astype(jnp.float32), axis=2)).reshape(TOKENS, D)
    block_result_entries = (values_f + summed_f).astype(jnp.bfloat16)
    picked_b = jax.vmap(pick_rows)(out_b, jnp.minimum(plan_b[0], slots - 1))
    normed_grad = lax.optimization_barrier(jnp.sum(plan_b[1][..., None] * picked_b.astype(jnp.float32), axis=2)).reshape(TOKENS, D)
    scaled = scaling * normed_grad
    inner = lax.optimization_barrier(jnp.mean(values_b * scaled, axis=-1, keepdims=True))
    block_source_derivative = grad_y.astype(jnp.float32) + inverse_b * scaled - values_b * inverse_b * inverse_b * inverse_b * inner
    return (block_result_entries, block_source_derivative.astype(jnp.bfloat16))

def reference(onward_block_activation, reverse_stored_activation, reverse_result_derivative, onward_specialist_choices, reverse_specialist_choices, onward_mixing_coefficients, reverse_mixing_coefficients, quota_table, rescaling_factor_list, gating_projection_matrix, expansion_matrix, contraction_matrix):
    forward_list = []
    gradient_list = []
    for segment_index in range(SECTIONS):
        block_result_entries, block_source_derivative = segment_clock_sweep(onward_block_activation[segment_index], reverse_stored_activation[segment_index], reverse_result_derivative[segment_index], onward_specialist_choices[segment_index], reverse_specialist_choices[segment_index], onward_mixing_coefficients[segment_index], reverse_mixing_coefficients[segment_index], quota_table[segment_index], rescaling_factor_list[segment_index], gating_projection_matrix[segment_index], expansion_matrix[segment_index], contraction_matrix[segment_index])
        forward_list.append(block_result_entries)
        gradient_list.append(block_source_derivative)
    fwd_next = jnp.roll(jnp.stack(forward_list), 1, axis=0)
    grad_next = jnp.roll(jnp.stack(gradient_list), -1, axis=0)
    return (fwd_next, grad_next)
```

```python
import jax
import jax.numpy as jnp
from jax import lax
from jax.sharding import PartitionSpec as P

CAP = 32


EPSILON = 1e-06


def passed_along(value, axis, steps):
    count = lax.axis_size(axis)
    pairs = [(source, (source + steps) % count) for source in range(count)]
    return lax.ppermute(value, axis, pairs)


def inverse_rms(values):
    return lax.rsqrt(jnp.mean(values * values, axis=-1, keepdims=True) + EPSILON)


def slot_map(routes, quota):
    count, tokens = quota.shape[0], routes.shape[0]
    chosen = routes.T
    experts = lax.broadcasted_iota(jnp.int32, (count, tokens), 0)
    first = experts == chosen[0][None, :]
    second = experts == chosen[1][None, :]
    named = first.astype(jnp.bfloat16) + second.astype(jnp.bfloat16)
    row = lax.broadcasted_iota(jnp.int32, (tokens, tokens), 0)
    column = lax.broadcasted_iota(jnp.int32, (tokens, tokens), 1)
    before = jnp.dot(
        named, (row < column).astype(jnp.bfloat16), preferred_element_type=jnp.float32
    ).astype(jnp.int32)

    def slot(mask, ranks, ids):
        rank = jnp.sum(jnp.where(mask, ranks, 0), axis=0)
        limit = jnp.sum(jnp.where(mask, quota[:, None], 0), axis=0)
        return jnp.where(rank < limit, ids * CAP + rank, -1)

    slot_first = slot(first, before, chosen[0])
    slot_second = slot(second, before + first.astype(jnp.int32), chosen[1])
    slots = lax.broadcasted_iota(jnp.int32, (count * CAP, tokens), 0)
    return slots == slot_first[None, :], slots == slot_second[None, :]


def weighted(masks, weights):
    return jnp.where(masks[0], weights[:, 0][None, :], 0.0) + jnp.where(
        masks[1], weights[:, 1][None, :], 0.0
    )


def to_slots(masks, rows):
    place = (masks[0] | masks[1]).astype(jnp.bfloat16)
    return jnp.dot(place, rows, preferred_element_type=jnp.float32)


def from_slots(place, table):
    return lax.dot_general(
        place, table, (((0,), (0,)), ((), ())), preferred_element_type=jnp.float32
    )


def exchange(rows):
    return lax.all_to_all(rows, "expert", split_axis=0, concat_axis=0, tiled=True)


def on_device(
    onward_block_activation,
    reverse_stored_activation,
    reverse_result_derivative,
    onward_specialist_choices,
    reverse_specialist_choices,
    onward_mixing_coefficients,
    reverse_mixing_coefficients,
    quota_table,
    rescaling_factor_list,
    gating_projection_matrix,
    expansion_matrix,
    contraction_matrix,
):
    f32, bf16 = jnp.float32, jnp.bfloat16
    contract = (((1,), (1,)), ((), ()))
    scaling = rescaling_factor_list[0]
    gate_w = gating_projection_matrix[0, 0]
    up_w = expansion_matrix[0, 0]
    down_w = contraction_matrix[0, 0]
    quota = quota_table[0]
    masks_b = slot_map(reverse_specialist_choices[0], quota)
    masks_f = slot_map(onward_specialist_choices[0], quota)

    grad_y = reverse_result_derivative[0]
    scale_b = jnp.sum(weighted(masks_b, reverse_mixing_coefficients[0]), axis=1, keepdims=True)
    grads = exchange((scale_b * to_slots(masks_b, grad_y)).astype(bf16))

    values_b = reverse_stored_activation[0].astype(f32)
    inverse_b = inverse_rms(values_b)
    normed_b = (values_b * inverse_b * scaling).astype(bf16)
    rows_b = exchange(to_slots(masks_b, normed_b).astype(bf16))

    values_f = onward_block_activation[0].astype(f32)
    normed_f = (values_f * inverse_rms(values_f) * scaling).astype(bf16)
    rows_f = exchange(to_slots(masks_f, normed_f).astype(bf16))

    hidden_grad = lax.dot_general(grads, down_w, contract, preferred_element_type=f32)
    gate_pre = jnp.dot(rows_b, gate_w, preferred_element_type=f32)
    up_pre = jnp.dot(rows_b, up_w, preferred_element_type=f32)
    sig = jax.nn.sigmoid(gate_pre)
    gate_grad = (hidden_grad * up_pre * sig * (1.0 + gate_pre * (1.0 - sig))).astype(bf16)
    up_grad = (hidden_grad * gate_pre * sig).astype(bf16)
    out_b = lax.dot_general(gate_grad, gate_w, contract, preferred_element_type=f32)
    out_b = out_b + lax.dot_general(up_grad, up_w, contract, preferred_element_type=f32)
    table_b = exchange(out_b.astype(bf16))

    gate_f = jnp.dot(rows_f, gate_w, preferred_element_type=f32)
    up_f = jnp.dot(rows_f, up_w, preferred_element_type=f32)
    hidden = (jax.nn.silu(gate_f) * up_f).astype(bf16)
    out_f = jnp.dot(hidden, down_w, preferred_element_type=f32).astype(bf16)
    table_f = exchange(out_f)

    place_b = (masks_b[0] | masks_b[1]).astype(bf16)
    scaled = scaling * from_slots(place_b, table_b)
    inner = jnp.mean(values_b * scaled, axis=-1, keepdims=True)
    grad = grad_y.astype(f32) + inverse_b * scaled - values_b * (inverse_b * inverse_b * inverse_b * inner)
    grad_next = passed_along(grad.astype(bf16), "pipe", -1)

    place_f = weighted(masks_f, onward_mixing_coefficients[0])
    high = place_f.astype(bf16)
    low = (place_f - high.astype(f32)).astype(bf16)
    summed = from_slots(high, table_f) + from_slots(low, table_f)
    fwd_next = passed_along((values_f + summed).astype(bf16), "pipe", 1)
    return (fwd_next[None], grad_next[None])


def solution(mesh):
    blocks = P("pipe", "expert", None)
    in_specs = (blocks,) * 7 + (P("pipe", None),) * 2 + (P("pipe", "expert", None, None),) * 3
    return jax.shard_map(
        on_device, mesh=mesh, in_specs=in_specs, out_specs=(blocks, blocks), check_vma=False
    )
```

```python
import functools

import jax
import jax.numpy as jnp
from jax import lax
from jax.experimental import pallas as pl
from jax.experimental.pallas import tpu as pltpu
from jax.sharding import PartitionSpec as P

CAP = 32
EPSILON = 1e-06
VMEM_LIMIT = 56 * 1024 * 1024
f32, bf16 = jnp.float32, jnp.bfloat16
ANY = pl.BlockSpec(memory_space=pl.ANY)


def params(steps):
    return pltpu.CompilerParams(
        dimension_semantics=("arbitrary",) * steps, vmem_limit_bytes=VMEM_LIMIT
    )


def cost(flops, moved_bytes):
    return pl.CostEstimate(flops=flops, bytes_accessed=moved_bytes, transcendentals=0)


def whole(shape):
    return pl.BlockSpec(shape, lambda *_: (0,) * len(shape))


def passed_along(value, axis, steps):
    count = lax.axis_size(axis)
    pairs = [(source, (source + steps) % count) for source in range(count)]
    return lax.ppermute(value, axis, pairs)


def inverse_rms(values):
    return lax.rsqrt(jnp.mean(values * values, axis=-1, keepdims=True) + EPSILON)


def after(value, *others):
    return lax.optimization_barrier((value, *others))[0]


def slots_of(chosen, quota):
    count, tokens = quota.shape[0], chosen.shape[1]
    experts = lax.broadcasted_iota(jnp.int32, (count, tokens), 0)
    first = experts == chosen[0][None, :]
    second = experts == chosen[1][None, :]
    named = first.astype(bf16) + second.astype(bf16)
    row = lax.broadcasted_iota(jnp.int32, (tokens, tokens), 0)
    column = lax.broadcasted_iota(jnp.int32, (tokens, tokens), 1)
    before = jnp.dot(
        named, (row < column).astype(bf16), preferred_element_type=f32
    ).astype(jnp.int32)

    def slot(mask, ranks, ids):
        rank = jnp.sum(jnp.where(mask, ranks, 0), axis=0)
        limit = jnp.sum(jnp.where(mask, quota[:, None], 0), axis=0)
        return jnp.where(rank < limit, ids * CAP + rank, -1)

    return jnp.stack(
        [
            slot(first, before, chosen[0]),
            slot(second, before + first.astype(jnp.int32), chosen[1]),
        ]
    )


def masks(place, count):
    rows = lax.broadcasted_iota(jnp.int32, (count, place.shape[1]), 0)
    return rows == place[0:1, :], rows == place[1:2, :]


def dispatch_kernel(place_ref, weight_ref, inverse_ref, scaling_ref, values_ref, grad_ref, out):
    count, rows_each, tile = out.shape
    first, second = masks(place_ref[...], count * CAP)
    chosen = jnp.where(first | second, 1.0, 0.0).astype(bf16)
    normed = values_ref[...].astype(f32) * inverse_ref[...] * scaling_ref[...]
    rows = jnp.dot(chosen, normed.astype(bf16), preferred_element_type=f32)
    out[:, :CAP, :] = rows.astype(bf16).reshape(count, CAP, tile)
    if rows_each > CAP:
        weight = weight_ref[...]
        scale = jnp.where(first, weight[0:1, :], 0.0) + jnp.where(second, weight[1:2, :], 0.0)
        rows = jnp.dot(chosen, grad_ref[...], preferred_element_type=f32)
        rows = rows * jnp.sum(scale, axis=1, keepdims=True)
        out[:, CAP:, :] = rows.astype(bf16).reshape(count, CAP, tile)


def dispatch(count, place, weight, inverse, scaling, values, grad):
    tokens, width = values.shape
    tile = 1024
    rows_each = CAP if grad is None else 2 * CAP
    column = pl.BlockSpec((tokens, tile), lambda i: (0, i))
    return pl.pallas_call(
        dispatch_kernel,
        grid=(width // tile,),
        in_specs=[
            whole(place.shape),
            whole(weight.shape),
            whole(inverse.shape),
            pl.BlockSpec((1, tile), lambda i: (0, i)),
            column,
            column,
        ],
        out_specs=pl.BlockSpec((count, rows_each, tile), lambda i: (0, 0, i)),
        out_shape=jax.ShapeDtypeStruct((count, rows_each, width), bf16),
        compiler_params=params(1),
        cost_estimate=cost(2 * count * rows_each * tokens * width, 2 * (count * rows_each + 2 * tokens) * width),
    )(place, weight, inverse, scaling, values, values if grad is None else grad)


CHUNK = 256


def load(source, start, rows, semaphore):
    copy = pltpu.make_async_copy(source.at[:, pl.ds(start, CAP), :], rows, semaphore)
    copy.start()
    copy.wait()


def chunk_of(rows, at):
    blocks = CHUNK // CAP
    return rows[pl.ds(at * blocks, blocks)].reshape(CHUNK, rows.shape[2])


def forward_kernel(tiles, source, gate_w, up_w, down_w, out, rows, hidden, semaphore):
    step = pl.program_id(0)

    @pl.when(step == 0)
    def _():
        load(source, 0, rows, semaphore)

    for index in range(tiles):

        @pl.when(step == index)
        def _():
            @pl.loop(0, hidden.shape[0] // CHUNK)
            def _(at):
                span = pl.ds(pl.multiple_of(at * CHUNK, CHUNK), CHUNK)
                values = chunk_of(rows, at)
                gate = jnp.dot(values, gate_w[...], preferred_element_type=f32)
                up = jnp.dot(values, up_w[...], preferred_element_type=f32)
                size = gate_w.shape[1]
                value = gate / (1.0 + jnp.exp(-gate)) * up
                hidden[span, index * size : (index + 1) * size] = value.astype(bf16)

    @pl.when(step >= tiles)
    def _():
        out[...] = jnp.dot(hidden[...], down_w[...], preferred_element_type=f32).astype(bf16)


def expert_forward(source, gate_w, up_w, down_w):
    width, hid = gate_w.shape
    total = source.shape[0] * CAP
    tile, out_tile = 256, 1024
    tiles, out_tiles = hid // tile, width // out_tile
    project = pl.BlockSpec((width, tile), lambda i: (0, jnp.minimum(i, tiles - 1)))
    late = lambda i: (0, jnp.maximum(i - tiles, 0))
    return pl.pallas_call(
        functools.partial(forward_kernel, tiles),
        grid=(tiles + out_tiles,),
        in_specs=[ANY, project, project, pl.BlockSpec((hid, out_tile), late)],
        out_specs=pl.BlockSpec((total, out_tile), late),
        out_shape=jax.ShapeDtypeStruct((total, width), bf16),
        scratch_shapes=[
            pltpu.VMEM((source.shape[0], CAP, width), bf16),
            pltpu.VMEM((total, hid), bf16),
            pltpu.SemaphoreType.DMA,
        ],
        compiler_params=params(1),
        cost_estimate=cost(6 * total * width * hid, 6 * width * hid + 4 * total * width),
    )(source, gate_w, up_w, down_w)


def hidden_grad_kernel(source, down_w, out, rows, semaphore):
    @pl.when(pl.program_id(0) == 0)
    def _():
        load(source, CAP, rows, semaphore)

    @pl.loop(0, out.shape[0] // CHUNK)
    def _(at):
        span = pl.ds(pl.multiple_of(at * CHUNK, CHUNK), CHUNK)
        out[span, :] = lax.dot_general(
            chunk_of(rows, at), down_w[...], (((1,), (1,)), ((), ())), preferred_element_type=f32
        )


def expert_hidden_grad(source, down_w):
    hid, width = down_w.shape
    total = source.shape[0] * CAP
    tile = 256
    return pl.pallas_call(
        hidden_grad_kernel,
        grid=(hid // tile,),
        in_specs=[ANY, pl.BlockSpec((tile, width), lambda i: (i, 0))],
        out_specs=pl.BlockSpec((total, tile), lambda i: (0, i)),
        out_shape=jax.ShapeDtypeStruct((total, hid), f32),
        scratch_shapes=[pltpu.VMEM((source.shape[0], CAP, width), bf16), pltpu.SemaphoreType.DMA],
        compiler_params=params(1),
        cost_estimate=cost(2 * total * width * hid, 2 * width * hid + 2 * total * width),
    )(source, down_w)


def gate_grads_kernel(source, gate_w, up_w, hidden_ref, gate_out, up_out, rows, semaphore):
    @pl.when(pl.program_id(0) == 0)
    def _():
        load(source, 0, rows, semaphore)

    @pl.loop(0, gate_out.shape[0] // CHUNK)
    def _(at):
        span = pl.ds(pl.multiple_of(at * CHUNK, CHUNK), CHUNK)
        values = chunk_of(rows, at)
        gate = jnp.dot(values, gate_w[...], preferred_element_type=f32)
        up = jnp.dot(values, up_w[...], preferred_element_type=f32)
        hidden_grad = hidden_ref[span, :]
        sig = 1.0 / (1.0 + jnp.exp(-gate))
        gate_out[span, :] = (hidden_grad * up * sig * (1.0 + gate * (1.0 - sig))).astype(bf16)
        up_out[span, :] = (hidden_grad * gate * sig).astype(bf16)


def expert_gate_grads(source, gate_w, up_w, hidden_grad):
    width, hid = gate_w.shape
    total = source.shape[0] * CAP
    tile = 256
    project = pl.BlockSpec((width, tile), lambda i: (0, i))
    column = pl.BlockSpec((total, tile), lambda i: (0, i))
    return pl.pallas_call(
        gate_grads_kernel,
        grid=(hid // tile,),
        in_specs=[ANY, project, project, column],
        out_specs=[column, column],
        out_shape=[jax.ShapeDtypeStruct((total, hid), bf16)] * 2,
        scratch_shapes=[pltpu.VMEM((source.shape[0], CAP, width), bf16), pltpu.SemaphoreType.DMA],
        compiler_params=params(1),
        cost_estimate=cost(4 * total * width * hid, 4 * width * hid + 2 * total * width + 8 * total * hid),
    )(source, gate_w, up_w, hidden_grad)


def entry_grads_kernel(gate_grad, up_grad, gate_w, up_w, out):
    contract = (((1,), (1,)), ((), ()))

    @pl.loop(0, gate_grad.shape[0] // CHUNK)
    def _(at):
        span = pl.ds(pl.multiple_of(at * CHUNK, CHUNK), CHUNK)
        rows = lax.dot_general(gate_grad[span, :], gate_w[...], contract, preferred_element_type=f32)
        rows = rows + lax.dot_general(up_grad[span, :], up_w[...], contract, preferred_element_type=f32)
        out[span, :] = rows.astype(bf16)


def expert_entry_grads(gate_grad, up_grad, gate_w, up_w, part, parts):
    total, hid = gate_grad.shape
    width = gate_w.shape[0] // parts
    tile = 512
    steps = width // tile
    weights = pl.BlockSpec((tile, hid), lambda i: (part * steps + i, 0))
    return pl.pallas_call(
        entry_grads_kernel,
        grid=(steps,),
        in_specs=[whole(gate_grad.shape), whole(up_grad.shape), weights, weights],
        out_specs=pl.BlockSpec((total, tile), lambda i: (0, i)),
        out_shape=jax.ShapeDtypeStruct((total, width), bf16),
        compiler_params=params(1),
        cost_estimate=cost(4 * total * width * hid, 4 * width * hid + 2 * total * width + 4 * total * hid),
    )(gate_grad, up_grad, gate_w, up_w)


def exchange(pieces):
    return lax.all_to_all(pieces, "expert", split_axis=0, concat_axis=0, tiled=True)


def from_slots(place, table):
    return lax.dot_general(place, table, (((0,), (0,)), ((), ())), preferred_element_type=f32)


def on_device(
    onward_block_activation,
    reverse_stored_activation,
    reverse_result_derivative,
    onward_specialist_choices,
    reverse_specialist_choices,
    onward_mixing_coefficients,
    reverse_mixing_coefficients,
    quota_table,
    rescaling_factor_list,
    gating_projection_matrix,
    expansion_matrix,
    contraction_matrix,
):
    scaling = rescaling_factor_list[0]
    gate_w = gating_projection_matrix[0, 0]
    up_w = expansion_matrix[0, 0]
    down_w = contraction_matrix[0, 0]
    quota = quota_table[0]
    count, width = quota.shape[0], gate_w.shape[0]
    input_f, input_b, grad_y = onward_block_activation[0], reverse_stored_activation[0], reverse_result_derivative[0]
    weight_f, weight_b = onward_mixing_coefficients[0].T, reverse_mixing_coefficients[0].T
    slots_f = slots_of(onward_specialist_choices[0].T, quota)
    slots_b = slots_of(reverse_specialist_choices[0].T, quota)
    values_f, values_b = input_f.astype(f32), input_b.astype(f32)
    inverse_f, inverse_b = inverse_rms(values_f), inverse_rms(values_b)

    send_f = dispatch(count, slots_f, weight_f, inverse_f, scaling[None], input_f, None)
    send_b = dispatch(count, slots_b, weight_b, inverse_b, scaling[None], input_b, grad_y)
    rows_f = exchange(send_f)
    rows_b = exchange(after(send_b, rows_f))

    out_f = expert_forward(rows_f, gate_w, up_w, down_w)
    table_f = exchange(after(out_f, rows_b).reshape(count, CAP, width)).reshape(count * CAP, width)

    hidden_grad = expert_hidden_grad(rows_b, down_w)
    gate_grad, up_grad = expert_gate_grads(rows_b, gate_w, up_w, hidden_grad)
    out_b = expert_entry_grads(gate_grad, up_grad, gate_w, up_w, 0, 1)
    table_b = exchange(after(out_b, table_f).reshape(count, CAP, width)).reshape(count * CAP, width)

    first, second = masks(slots_f, count * CAP)
    mixed = jnp.where(first, weight_f[0:1, :], 0.0) + jnp.where(second, weight_f[1:2, :], 0.0)
    high = mixed.astype(bf16)
    low = (mixed - high.astype(f32)).astype(bf16)
    fwd = values_f + from_slots(high, table_f) + from_slots(low, table_f)
    fwd_next = passed_along(fwd.astype(bf16), "pipe", 1)

    first, second = masks(slots_b, count * CAP)
    scaled = scaling * from_slots((first | second).astype(bf16), table_b)
    inner = jnp.mean(values_b * scaled, axis=-1, keepdims=True)
    grad = grad_y.astype(f32) + inverse_b * scaled
    grad = grad - values_b * (inverse_b * inverse_b * inverse_b * inner)
    grad_next = passed_along(grad.astype(bf16), "pipe", -1)
    return (fwd_next[None], grad_next[None])


def solution(mesh):
    blocks = P("pipe", "expert", None)
    in_specs = (blocks,) * 7 + (P("pipe", None),) * 2 + (P("pipe", "expert", None, None),) * 3
    return jax.shard_map(
        on_device, mesh=mesh, in_specs=in_specs, out_specs=(blocks, blocks), check_vma=False
    )
```

```python
import functools

import jax
import jax.numpy as jnp
from jax import lax
from jax.experimental import pallas as pl
from jax.experimental.pallas import tpu as pltpu
from jax.sharding import PartitionSpec as P

CAP = 32
EPSILON = 1e-06
VMEM_LIMIT = 56 * 1024 * 1024
f32, bf16 = jnp.float32, jnp.bfloat16
ANY = pl.BlockSpec(memory_space=pl.ANY)


def params(steps):
    return pltpu.CompilerParams(
        dimension_semantics=("arbitrary",) * steps, vmem_limit_bytes=VMEM_LIMIT
    )


def cost(flops, moved_bytes):
    return pl.CostEstimate(flops=flops, bytes_accessed=moved_bytes, transcendentals=0)


def whole(shape):
    return pl.BlockSpec(shape, lambda *_: (0,) * len(shape))


def passed_along(value, axis, steps):
    count = lax.axis_size(axis)
    pairs = [(source, (source + steps) % count) for source in range(count)]
    return lax.ppermute(value, axis, pairs)


def after(value, *others):
    return lax.optimization_barrier((value, *others))[0]


def masks(place, count):
    rows = lax.broadcasted_iota(jnp.int32, (count, place.shape[1]), 0)
    return rows == place[0:1, :], rows == place[1:2, :]


def slots_of(chosen, quota, count):
    tokens = chosen.shape[1]
    first, second = masks(chosen, count)
    first, second = jnp.where(first, 1.0, 0.0), jnp.where(second, 1.0, 0.0)
    row = lax.broadcasted_iota(jnp.int32, (tokens, tokens), 0)
    column = lax.broadcasted_iota(jnp.int32, (tokens, tokens), 1)
    earlier = jnp.where(row < column, 1.0, 0.0).astype(bf16)
    before = jnp.dot((first + second).astype(bf16), earlier, preferred_element_type=f32)
    slots = []
    for at, (mask, ranks) in enumerate(((first, before), (second, before + first))):
        ids = chosen[at : at + 1, :]
        rank = jnp.sum(mask * ranks, axis=0, keepdims=True).astype(jnp.int32)
        limit = jnp.zeros_like(ids)
        for expert in range(count):
            limit = jnp.where(ids == expert, quota[0, expert], limit)
        slots.append(jnp.where(rank < limit, ids * CAP + rank, -1))
    return slots


def dispatch_kernel(has_grad, quota, chosen_ref, weight_ref, scaling_ref, values_ref, *refs):
    grad_ref, (out, place_ref, inverse_ref) = refs[0], refs[-3:]
    count, _, tile = out.shape
    step = pl.program_id(0)

    @pl.when(step == 0)
    def _():
        values = values_ref[...].astype(f32)
        inverse_ref[...] = lax.rsqrt(jnp.mean(values * values, axis=1, keepdims=True) + EPSILON)
        first, second = slots_of(chosen_ref[...], quota, count)
        place_ref[0:1, :] = first
        place_ref[1:2, :] = second

    first, second = masks(place_ref[...], count * CAP)
    chosen = jnp.where(first | second, 1.0, 0.0).astype(bf16)
    values = values_ref[:, pl.ds(pl.multiple_of(step * tile, tile), tile)].astype(f32)
    normed = (values * inverse_ref[...] * scaling_ref[...]).astype(bf16)
    rows = jnp.dot(chosen, normed, preferred_element_type=f32)
    out[:, :CAP, :] = rows.astype(bf16).reshape(count, CAP, tile)
    if has_grad:
        weight = weight_ref[...]
        scale = jnp.where(first, weight[0:1, :], 0.0) + jnp.where(second, weight[1:2, :], 0.0)
        rows = jnp.dot(chosen, grad_ref[...], preferred_element_type=f32)
        rows = rows * jnp.sum(scale, axis=1, keepdims=True)
        out[:, CAP:, :] = rows.astype(bf16).reshape(count, CAP, tile)


def dispatch(quota, chosen, weight, scaling, values, grad=None):
    count, (tokens, width) = quota.shape[1], values.shape
    tile = 1024
    rows_each = CAP if grad is None else 2 * CAP
    column = pl.BlockSpec((tokens, tile), lambda i: (0, i))
    return pl.pallas_call(
        functools.partial(dispatch_kernel, grad is not None),
        grid=(width // tile,),
        in_specs=[
            pl.BlockSpec(memory_space=pltpu.SMEM),
            whole(chosen.shape),
            whole(weight.shape),
            pl.BlockSpec((1, tile), lambda i: (0, i)),
            whole(values.shape),
        ]
        + [column] * (grad is not None),
        out_specs=[
            pl.BlockSpec((count, rows_each, tile), lambda i: (0, 0, i)),
            whole(chosen.shape),
            whole((tokens, 1)),
        ],
        out_shape=[
            jax.ShapeDtypeStruct((count, rows_each, width), bf16),
            jax.ShapeDtypeStruct(chosen.shape, jnp.int32),
            jax.ShapeDtypeStruct((tokens, 1), f32),
        ],
        compiler_params=params(1),
        cost_estimate=cost(2 * count * rows_each * tokens * width, 2 * (count * rows_each + 2 * tokens) * width),
    )(quota, chosen, weight, scaling, values, *([] if grad is None else [grad]))


CHUNK = 256


def load(source, start, rows, semaphore):
    copy = pltpu.make_async_copy(source.at[:, pl.ds(start, CAP), :], rows, semaphore)
    copy.start()
    copy.wait()


def chunk_of(rows, at):
    blocks = CHUNK // CAP
    return rows[pl.ds(at * blocks, blocks)].reshape(CHUNK, rows.shape[2])


def forward_kernel(tiles, source, gate_w, up_w, down_w, out, rows, hidden, semaphore):
    step = pl.program_id(0)

    @pl.when(step == 0)
    def _():
        load(source, 0, rows, semaphore)

    for index in range(tiles):

        @pl.when(step == index)
        def _():
            @pl.loop(0, hidden.shape[0] // CHUNK)
            def _(at):
                span = pl.ds(pl.multiple_of(at * CHUNK, CHUNK), CHUNK)
                values = chunk_of(rows, at)
                gate = jnp.dot(values, gate_w[...], preferred_element_type=f32)
                up = jnp.dot(values, up_w[...], preferred_element_type=f32)
                size = gate_w.shape[1]
                value = gate / (1.0 + jnp.exp(-gate)) * up
                hidden[span, index * size : (index + 1) * size] = value.astype(bf16)

    @pl.when(step >= tiles)
    def _():
        out[...] = jnp.dot(hidden[...], down_w[...], preferred_element_type=f32).astype(bf16)


def expert_forward(source, gate_w, up_w, down_w):
    width, hid = gate_w.shape
    total = source.shape[0] * CAP
    tile, out_tile = 256, 1024
    tiles, out_tiles = hid // tile, width // out_tile
    project = pl.BlockSpec((width, tile), lambda i: (0, jnp.minimum(i, tiles - 1)))
    late = lambda i: (0, jnp.maximum(i - tiles, 0))
    return pl.pallas_call(
        functools.partial(forward_kernel, tiles),
        grid=(tiles + out_tiles,),
        in_specs=[ANY, project, project, pl.BlockSpec((hid, out_tile), late)],
        out_specs=pl.BlockSpec((total, out_tile), late),
        out_shape=jax.ShapeDtypeStruct((total, width), bf16),
        scratch_shapes=[
            pltpu.VMEM((source.shape[0], CAP, width), bf16),
            pltpu.VMEM((total, hid), bf16),
            pltpu.SemaphoreType.DMA,
        ],
        compiler_params=params(1),
        cost_estimate=cost(6 * total * width * hid, 6 * width * hid + 4 * total * width),
    )(source, gate_w, up_w, down_w)


def hidden_grad_kernel(source, down_w, out, rows, semaphore):
    @pl.when(pl.program_id(0) == 0)
    def _():
        load(source, CAP, rows, semaphore)

    @pl.loop(0, out.shape[0] // CHUNK)
    def _(at):
        span = pl.ds(pl.multiple_of(at * CHUNK, CHUNK), CHUNK)
        out[span, :] = lax.dot_general(
            chunk_of(rows, at), down_w[...], (((1,), (1,)), ((), ())), preferred_element_type=f32
        )


def expert_hidden_grad(source, down_w):
    hid, width = down_w.shape
    total = source.shape[0] * CAP
    tile = 256
    return pl.pallas_call(
        hidden_grad_kernel,
        grid=(hid // tile,),
        in_specs=[ANY, pl.BlockSpec((tile, width), lambda i: (i, 0))],
        out_specs=pl.BlockSpec((total, tile), lambda i: (0, i)),
        out_shape=jax.ShapeDtypeStruct((total, hid), f32),
        scratch_shapes=[pltpu.VMEM((source.shape[0], CAP, width), bf16), pltpu.SemaphoreType.DMA],
        compiler_params=params(1),
        cost_estimate=cost(2 * total * width * hid, 2 * width * hid + 2 * total * width),
    )(source, down_w)


def gate_grads_kernel(source, gate_w, up_w, hidden_ref, gate_out, up_out, rows, semaphore):
    @pl.when(pl.program_id(0) == 0)
    def _():
        load(source, 0, rows, semaphore)

    @pl.loop(0, gate_out.shape[0] // CHUNK)
    def _(at):
        span = pl.ds(pl.multiple_of(at * CHUNK, CHUNK), CHUNK)
        values = chunk_of(rows, at)
        gate = jnp.dot(values, gate_w[...], preferred_element_type=f32)
        up = jnp.dot(values, up_w[...], preferred_element_type=f32)
        hidden_grad = hidden_ref[span, :]
        sig = 1.0 / (1.0 + jnp.exp(-gate))
        gate_out[span, :] = (hidden_grad * up * sig * (1.0 + gate * (1.0 - sig))).astype(bf16)
        up_out[span, :] = (hidden_grad * gate * sig).astype(bf16)


def expert_gate_grads(source, gate_w, up_w, hidden_grad):
    width, hid = gate_w.shape
    total = source.shape[0] * CAP
    tile = 256
    project = pl.BlockSpec((width, tile), lambda i: (0, i))
    column = pl.BlockSpec((total, tile), lambda i: (0, i))
    return pl.pallas_call(
        gate_grads_kernel,
        grid=(hid // tile,),
        in_specs=[ANY, project, project, column],
        out_specs=[column, column],
        out_shape=[jax.ShapeDtypeStruct((total, hid), bf16)] * 2,
        scratch_shapes=[pltpu.VMEM((source.shape[0], CAP, width), bf16), pltpu.SemaphoreType.DMA],
        compiler_params=params(1),
        cost_estimate=cost(4 * total * width * hid, 4 * width * hid + 2 * total * width + 8 * total * hid),
    )(source, gate_w, up_w, hidden_grad)


def entry_grads_kernel(gate_grad, up_grad, gate_w, up_w, out):
    contract = (((1,), (1,)), ((), ()))

    @pl.loop(0, gate_grad.shape[0] // CHUNK)
    def _(at):
        span = pl.ds(pl.multiple_of(at * CHUNK, CHUNK), CHUNK)
        rows = lax.dot_general(gate_grad[span, :], gate_w[...], contract, preferred_element_type=f32)
        rows = rows + lax.dot_general(up_grad[span, :], up_w[...], contract, preferred_element_type=f32)
        out[span, :] = rows.astype(bf16)


def expert_entry_grads(gate_grad, up_grad, gate_w, up_w, part, parts):
    total, hid = gate_grad.shape
    width = gate_w.shape[0] // parts
    tile = 512
    steps = width // tile
    weights = pl.BlockSpec((tile, hid), lambda i: (part * steps + i, 0))
    return pl.pallas_call(
        entry_grads_kernel,
        grid=(steps,),
        in_specs=[whole(gate_grad.shape), whole(up_grad.shape), weights, weights],
        out_specs=pl.BlockSpec((total, tile), lambda i: (0, i)),
        out_shape=jax.ShapeDtypeStruct((total, width), bf16),
        compiler_params=params(1),
        cost_estimate=cost(4 * total * width * hid, 4 * width * hid + 2 * total * width + 4 * total * hid),
    )(gate_grad, up_grad, gate_w, up_w)


def exchange(pieces):
    return lax.all_to_all(pieces, "expert", split_axis=0, concat_axis=0, tiled=True)


def from_slots(place, table):
    return lax.dot_general(place, table, (((0,), (0,)), ((), ())), preferred_element_type=f32)


def written_kernel(source, out):
    out[...] = source[...]


def written(rows):
    block = pl.BlockSpec((rows.shape[0] // 2, rows.shape[1]), lambda i: (i, 0))
    return pl.pallas_call(
        written_kernel,
        grid=(2,),
        in_specs=[block],
        out_specs=block,
        out_shape=jax.ShapeDtypeStruct(rows.shape, rows.dtype),
        compiler_params=params(1),
        cost_estimate=cost(0, 4 * rows.size),
    )(rows)


def on_device(
    onward_block_activation,
    reverse_stored_activation,
    reverse_result_derivative,
    onward_specialist_choices,
    reverse_specialist_choices,
    onward_mixing_coefficients,
    reverse_mixing_coefficients,
    quota_table,
    rescaling_factor_list,
    gating_projection_matrix,
    expansion_matrix,
    contraction_matrix,
):
    scaling = rescaling_factor_list
    gate_w = gating_projection_matrix[0, 0]
    up_w = expansion_matrix[0, 0]
    down_w = contraction_matrix[0, 0]
    count, width = quota_table.shape[1], gate_w.shape[0]
    input_f, input_b, grad_y = onward_block_activation[0], reverse_stored_activation[0], reverse_result_derivative[0]
    weight_f, weight_b = onward_mixing_coefficients[0].T, reverse_mixing_coefficients[0].T
    chosen_f, chosen_b = onward_specialist_choices[0].T, reverse_specialist_choices[0].T

    send_f, slots_f, _ = dispatch(quota_table, chosen_f, weight_f, scaling, input_f)
    rows_f = exchange(send_f)
    send_b, slots_b, inverse_b = dispatch(quota_table, chosen_b, weight_b, scaling, input_b, grad_y)
    rows_b = exchange(after(send_b, rows_f))

    out_f = expert_forward(rows_f, gate_w, up_w, down_w)
    table_f = exchange(after(out_f, rows_b).reshape(count, CAP, width)).reshape(count * CAP, width)
    hidden_grad = expert_hidden_grad(rows_b, down_w)
    gate_grad, up_grad = expert_gate_grads(rows_b, gate_w, up_w, hidden_grad)
    out_b = expert_entry_grads(gate_grad, up_grad, gate_w, up_w, 0, 1)
    table_b = exchange(after(out_b, table_f).reshape(count, CAP, width)).reshape(count * CAP, width)

    first, second = masks(slots_f, count * CAP)
    mixed = jnp.where(first, weight_f[0:1, :], 0.0) + jnp.where(second, weight_f[1:2, :], 0.0)
    high = mixed.astype(bf16)
    low = (mixed - high.astype(f32)).astype(bf16)
    fwd = input_f.astype(f32) + from_slots(high, table_f) + from_slots(low, table_f)
    fwd_next = passed_along(fwd.astype(bf16), "pipe", 1)

    first, second = masks(slots_b, count * CAP)
    scaled = scaling * from_slots((first | second).astype(bf16), table_b)
    values_b = input_b.astype(f32)
    inner = jnp.mean(values_b * scaled, axis=-1, keepdims=True)
    grad = grad_y.astype(f32) + inverse_b * scaled
    grad = grad - values_b * (inverse_b * inverse_b * inverse_b * inner)
    grad_next = passed_along(grad.astype(bf16), "pipe", -1)
    return (written(fwd_next)[None], grad_next[None])


def solution(mesh):
    blocks = P("pipe", "expert", None)
    in_specs = (blocks,) * 7 + (P("pipe", None),) * 2 + (P("pipe", "expert", None, None),) * 3
    return jax.shard_map(
        on_device, mesh=mesh, in_specs=in_specs, out_specs=(blocks, blocks), check_vma=False
    )
```

```python
import functools

import jax
import jax.numpy as jnp
from jax import lax
from jax.experimental import pallas as pl
from jax.experimental.pallas import tpu as pltpu
from jax.sharding import PartitionSpec as P

CAP = 32
EPSILON = 1e-06
VMEM_LIMIT = 56 * 1024 * 1024
f32, bf16 = jnp.float32, jnp.bfloat16
ANY = pl.BlockSpec(memory_space=pl.ANY)


def params(steps):
    return pltpu.CompilerParams(
        dimension_semantics=("arbitrary",) * steps, vmem_limit_bytes=VMEM_LIMIT
    )


def cost(flops, moved_bytes):
    return pl.CostEstimate(flops=flops, bytes_accessed=moved_bytes, transcendentals=0)


def whole(shape):
    return pl.BlockSpec(shape, lambda *_: (0,) * len(shape))


def passed_along(value, axis, steps):
    count = lax.axis_size(axis)
    pairs = [(source, (source + steps) % count) for source in range(count)]
    return lax.ppermute(value, axis, pairs)


def after(value, *others):
    return lax.optimization_barrier((value, *others))[0]


def masks(place, count):
    rows = lax.broadcasted_iota(jnp.int32, (count, place.shape[1]), 0)
    return rows == place[0:1, :], rows == place[1:2, :]


def slots_of(chosen, quota, count):
    tokens = chosen.shape[1]
    first, second = masks(chosen, count)
    first, second = jnp.where(first, 1.0, 0.0), jnp.where(second, 1.0, 0.0)
    row = lax.broadcasted_iota(jnp.int32, (tokens, tokens), 0)
    column = lax.broadcasted_iota(jnp.int32, (tokens, tokens), 1)
    earlier = jnp.where(row < column, 1.0, 0.0).astype(bf16)
    before = jnp.dot((first + second).astype(bf16), earlier, preferred_element_type=f32)
    slots = []
    for at, (mask, ranks) in enumerate(((first, before), (second, before + first))):
        ids = chosen[at : at + 1, :]
        rank = jnp.sum(mask * ranks, axis=0, keepdims=True).astype(jnp.int32)
        limit = jnp.zeros_like(ids)
        for expert in range(count):
            limit = jnp.where(ids == expert, quota[0, expert], limit)
        slots.append(jnp.where(rank < limit, ids * CAP + rank, -1))
    return slots


def dispatch_kernel(has_grad, quota, chosen_ref, weight_ref, scaling_ref, values_ref, *refs):
    grad_ref, (out, place_ref, inverse_ref, chosen, scale) = refs[0], refs[-5:]
    count, _, tile = out.shape
    step = pl.program_id(0)

    @pl.when(step == 0)
    def _():
        values = values_ref[...].astype(f32)
        inverse_ref[...] = lax.rsqrt(jnp.mean(values * values, axis=1, keepdims=True) + EPSILON)
        first, second = slots_of(chosen_ref[...], quota, count)
        place_ref[0:1, :] = first
        place_ref[1:2, :] = second
        first, second = masks(place_ref[...], count * CAP)
        chosen[...] = jnp.where(first | second, 1.0, 0.0).astype(bf16)
        if has_grad:
            weight = weight_ref[...]
            mixed = jnp.where(first, weight[0:1, :], 0.0) + jnp.where(second, weight[1:2, :], 0.0)
            scale[...] = jnp.sum(mixed, axis=1, keepdims=True)

    values = values_ref[:, pl.ds(pl.multiple_of(step * tile, tile), tile)].astype(f32)
    normed = (values * inverse_ref[...] * scaling_ref[...]).astype(bf16)
    rows = jnp.dot(chosen[...], normed, preferred_element_type=f32)
    out[:, :CAP, :] = rows.astype(bf16).reshape(count, CAP, tile)
    if has_grad:
        rows = jnp.dot(chosen[...], grad_ref[...], preferred_element_type=f32) * scale[...]
        out[:, CAP:, :] = rows.astype(bf16).reshape(count, CAP, tile)


def dispatch(quota, chosen, weight, scaling, values, grad=None):
    count, (tokens, width) = quota.shape[1], values.shape
    tile = 2048 if grad is None else 1024
    rows_each = CAP if grad is None else 2 * CAP
    column = pl.BlockSpec((tokens, tile), lambda i: (0, i))
    return pl.pallas_call(
        functools.partial(dispatch_kernel, grad is not None),
        grid=(width // tile,),
        in_specs=[
            pl.BlockSpec(memory_space=pltpu.SMEM),
            whole(chosen.shape),
            whole(weight.shape),
            pl.BlockSpec((1, tile), lambda i: (0, i)),
            whole(values.shape),
        ]
        + [column] * (grad is not None),
        out_specs=[
            pl.BlockSpec((count, rows_each, tile), lambda i: (0, 0, i)),
            whole(chosen.shape),
            whole((tokens, 1)),
        ],
        out_shape=[
            jax.ShapeDtypeStruct((count, rows_each, width), bf16),
            jax.ShapeDtypeStruct(chosen.shape, jnp.int32),
            jax.ShapeDtypeStruct((tokens, 1), f32),
        ],
        scratch_shapes=[
            pltpu.VMEM((count * CAP, tokens), bf16),
            pltpu.VMEM((count * CAP, 1), f32),
        ],
        compiler_params=params(1),
        cost_estimate=cost(2 * count * rows_each * tokens * width, 2 * (count * rows_each + 2 * tokens) * width),
    )(quota, chosen, weight, scaling, values, *([] if grad is None else [grad]))


CHUNK = 256


def load(source, start, rows, semaphore):
    copy = pltpu.make_async_copy(source.at[:, pl.ds(start, CAP), :], rows, semaphore)
    copy.start()
    copy.wait()


def chunk_of(rows, at):
    blocks = CHUNK // CAP
    return rows[pl.ds(at * blocks, blocks)].reshape(CHUNK, rows.shape[2])


def forward_kernel(tiles, source, gate_w, up_w, down_w, out, rows, hidden, semaphore):
    step = pl.program_id(0)

    @pl.when(step == 0)
    def _():
        load(source, 0, rows, semaphore)

    for index in range(tiles):

        @pl.when(step == index)
        def _():
            @pl.loop(0, hidden.shape[0] // CHUNK)
            def _(at):
                span = pl.ds(pl.multiple_of(at * CHUNK, CHUNK), CHUNK)
                values = chunk_of(rows, at)
                gate = jnp.dot(values, gate_w[...], preferred_element_type=f32)
                up = jnp.dot(values, up_w[...], preferred_element_type=f32)
                size = gate_w.shape[1]
                value = gate / (1.0 + jnp.exp(-gate)) * up
                hidden[span, index * size : (index + 1) * size] = value.astype(bf16)

    @pl.when(step >= tiles)
    def _():
        out[...] = jnp.dot(hidden[...], down_w[...], preferred_element_type=f32).astype(bf16)


def expert_forward(source, gate_w, up_w, down_w):
    width, hid = gate_w.shape
    total = source.shape[0] * CAP
    tile, out_tile = 256, 1024
    tiles, out_tiles = hid // tile, width // out_tile
    project = pl.BlockSpec((width, tile), lambda i: (0, jnp.minimum(i, tiles - 1)))
    late = lambda i: (0, jnp.maximum(i - tiles, 0))
    return pl.pallas_call(
        functools.partial(forward_kernel, tiles),
        grid=(tiles + out_tiles,),
        in_specs=[ANY, project, project, pl.BlockSpec((hid, out_tile), late)],
        out_specs=pl.BlockSpec((total, out_tile), late),
        out_shape=jax.ShapeDtypeStruct((total, width), bf16),
        scratch_shapes=[
            pltpu.VMEM((source.shape[0], CAP, width), bf16),
            pltpu.VMEM((total, hid), bf16),
            pltpu.SemaphoreType.DMA,
        ],
        compiler_params=params(1),
        cost_estimate=cost(6 * total * width * hid, 6 * width * hid + 4 * total * width),
    )(source, gate_w, up_w, down_w)


def hidden_grad_kernel(source, down_w, out, rows, semaphore):
    @pl.when(pl.program_id(0) == 0)
    def _():
        load(source, CAP, rows, semaphore)

    @pl.loop(0, out.shape[0] // CHUNK)
    def _(at):
        span = pl.ds(pl.multiple_of(at * CHUNK, CHUNK), CHUNK)
        out[span, :] = lax.dot_general(
            chunk_of(rows, at), down_w[...], (((1,), (1,)), ((), ())), preferred_element_type=f32
        )


def expert_hidden_grad(source, down_w):
    hid, width = down_w.shape
    total = source.shape[0] * CAP
    tile = 256
    return pl.pallas_call(
        hidden_grad_kernel,
        grid=(hid // tile,),
        in_specs=[ANY, pl.BlockSpec((tile, width), lambda i: (i, 0))],
        out_specs=pl.BlockSpec((total, tile), lambda i: (0, i)),
        out_shape=jax.ShapeDtypeStruct((total, hid), f32),
        scratch_shapes=[pltpu.VMEM((source.shape[0], CAP, width), bf16), pltpu.SemaphoreType.DMA],
        compiler_params=params(1),
        cost_estimate=cost(2 * total * width * hid, 2 * width * hid + 2 * total * width),
    )(source, down_w)


def gate_grads_kernel(source, gate_w, up_w, hidden_ref, gate_out, up_out, rows, semaphore):
    @pl.when(pl.program_id(0) == 0)
    def _():
        load(source, 0, rows, semaphore)

    @pl.loop(0, gate_out.shape[0] // CHUNK)
    def _(at):
        span = pl.ds(pl.multiple_of(at * CHUNK, CHUNK), CHUNK)
        values = chunk_of(rows, at)
        gate = jnp.dot(values, gate_w[...], preferred_element_type=f32)
        up = jnp.dot(values, up_w[...], preferred_element_type=f32)
        hidden_grad = hidden_ref[span, :]
        sig = 1.0 / (1.0 + jnp.exp(-gate))
        gate_out[span, :] = (hidden_grad * up * sig * (1.0 + gate * (1.0 - sig))).astype(bf16)
        up_out[span, :] = (hidden_grad * gate * sig).astype(bf16)


def expert_gate_grads(source, gate_w, up_w, hidden_grad):
    width, hid = gate_w.shape
    total = source.shape[0] * CAP
    tile = 256
    project = pl.BlockSpec((width, tile), lambda i: (0, i))
    column = pl.BlockSpec((total, tile), lambda i: (0, i))
    return pl.pallas_call(
        gate_grads_kernel,
        grid=(hid // tile,),
        in_specs=[ANY, project, project, column],
        out_specs=[column, column],
        out_shape=[jax.ShapeDtypeStruct((total, hid), bf16)] * 2,
        scratch_shapes=[pltpu.VMEM((source.shape[0], CAP, width), bf16), pltpu.SemaphoreType.DMA],
        compiler_params=params(1),
        cost_estimate=cost(4 * total * width * hid, 4 * width * hid + 2 * total * width + 8 * total * hid),
    )(source, gate_w, up_w, hidden_grad)


def entry_grads_kernel(gate_grad, up_grad, gate_w, up_w, out):
    contract = (((1,), (1,)), ((), ()))

    @pl.loop(0, gate_grad.shape[0] // CHUNK)
    def _(at):
        span = pl.ds(pl.multiple_of(at * CHUNK, CHUNK), CHUNK)
        rows = lax.dot_general(gate_grad[span, :], gate_w[...], contract, preferred_element_type=f32)
        rows = rows + lax.dot_general(up_grad[span, :], up_w[...], contract, preferred_element_type=f32)
        out[span, :] = rows.astype(bf16)


def expert_entry_grads(gate_grad, up_grad, gate_w, up_w, part, parts):
    total, hid = gate_grad.shape
    width = gate_w.shape[0] // parts
    tile = 512
    steps = width // tile
    weights = pl.BlockSpec((tile, hid), lambda i: (part * steps + i, 0))
    return pl.pallas_call(
        entry_grads_kernel,
        grid=(steps,),
        in_specs=[whole(gate_grad.shape), whole(up_grad.shape), weights, weights],
        out_specs=pl.BlockSpec((total, tile), lambda i: (0, i)),
        out_shape=jax.ShapeDtypeStruct((total, width), bf16),
        compiler_params=params(1),
        cost_estimate=cost(4 * total * width * hid, 4 * width * hid + 2 * total * width + 4 * total * hid),
    )(gate_grad, up_grad, gate_w, up_w)


def exchange(pieces):
    return lax.all_to_all(pieces, "expert", split_axis=0, concat_axis=0, tiled=True)


def from_slots(place, table):
    return lax.dot_general(place, table, (((0,), (0,)), ((), ())), preferred_element_type=f32)


def written_kernel(source, out):
    out[...] = source[...]


def written(rows):
    block = pl.BlockSpec((rows.shape[0] // 2, rows.shape[1]), lambda i: (i, 0))
    return pl.pallas_call(
        written_kernel,
        grid=(2,),
        in_specs=[block],
        out_specs=block,
        out_shape=jax.ShapeDtypeStruct(rows.shape, rows.dtype),
        compiler_params=params(1),
        cost_estimate=cost(0, 4 * rows.size),
    )(rows)


def on_device(
    onward_block_activation,
    reverse_stored_activation,
    reverse_result_derivative,
    onward_specialist_choices,
    reverse_specialist_choices,
    onward_mixing_coefficients,
    reverse_mixing_coefficients,
    quota_table,
    rescaling_factor_list,
    gating_projection_matrix,
    expansion_matrix,
    contraction_matrix,
):
    scaling = rescaling_factor_list
    gate_w = gating_projection_matrix[0, 0]
    up_w = expansion_matrix[0, 0]
    down_w = contraction_matrix[0, 0]
    count, width = quota_table.shape[1], gate_w.shape[0]
    input_f, input_b, grad_y = onward_block_activation[0], reverse_stored_activation[0], reverse_result_derivative[0]
    weight_f, weight_b = onward_mixing_coefficients[0].T, reverse_mixing_coefficients[0].T
    chosen_f, chosen_b = onward_specialist_choices[0].T, reverse_specialist_choices[0].T

    send_f, slots_f, _ = dispatch(quota_table, chosen_f, weight_f, scaling, input_f)
    rows_f = exchange(send_f)
    send_b, slots_b, inverse_b = dispatch(quota_table, chosen_b, weight_b, scaling, input_b, grad_y)
    rows_b = exchange(after(send_b, rows_f))

    out_f = expert_forward(rows_f, gate_w, up_w, down_w)
    table_f = exchange(after(out_f, rows_b).reshape(count, CAP, width)).reshape(count * CAP, width)
    hidden_grad = expert_hidden_grad(rows_b, down_w)
    gate_grad, up_grad = expert_gate_grads(rows_b, gate_w, up_w, hidden_grad)
    out_b = expert_entry_grads(gate_grad, up_grad, gate_w, up_w, 0, 1)
    table_b = exchange(after(out_b, table_f).reshape(count, CAP, width)).reshape(count * CAP, width)

    first, second = masks(slots_f, count * CAP)
    mixed = jnp.where(first, weight_f[0:1, :], 0.0) + jnp.where(second, weight_f[1:2, :], 0.0)
    high = mixed.astype(bf16)
    low = (mixed - high.astype(f32)).astype(bf16)
    fwd = input_f.astype(f32) + from_slots(high, table_f) + from_slots(low, table_f)
    fwd_next = passed_along(fwd.astype(bf16), "pipe", 1)

    first, second = masks(slots_b, count * CAP)
    scaled = scaling * from_slots((first | second).astype(bf16), table_b)
    values_b = input_b.astype(f32)
    inner = jnp.mean(values_b * scaled, axis=-1, keepdims=True)
    grad = grad_y.astype(f32) + inverse_b * scaled
    grad = grad - values_b * (inverse_b * inverse_b * inverse_b * inner)
    grad_next = passed_along(grad.astype(bf16), "pipe", -1)
    return (written(fwd_next)[None], grad_next[None])


def solution(mesh):
    blocks = P("pipe", "expert", None)
    in_specs = (blocks,) * 7 + (P("pipe", None),) * 2 + (P("pipe", "expert", None, None),) * 3
    return jax.shard_map(
        on_device, mesh=mesh, in_specs=in_specs, out_specs=(blocks, blocks), check_vma=False
    )
```

```python
import functools

import jax
import jax.numpy as jnp
from jax import lax
from jax.experimental import pallas as pl
from jax.experimental.pallas import tpu as pltpu
from jax.sharding import PartitionSpec as P

CAP = 32
EPSILON = 1e-06
VMEM_LIMIT = 56 * 1024 * 1024
f32, bf16 = jnp.float32, jnp.bfloat16
ANY = pl.BlockSpec(memory_space=pl.ANY)


def params(steps):
    return pltpu.CompilerParams(
        dimension_semantics=("arbitrary",) * steps, vmem_limit_bytes=VMEM_LIMIT
    )


def cost(flops, moved_bytes):
    return pl.CostEstimate(flops=flops, bytes_accessed=moved_bytes, transcendentals=0)


def whole(shape):
    return pl.BlockSpec(shape, lambda *_: (0,) * len(shape))


def passed_along(value, axis, steps):
    count = lax.axis_size(axis)
    pairs = [(source, (source + steps) % count) for source in range(count)]
    return lax.ppermute(value, axis, pairs)


def after(value, *others):
    return lax.optimization_barrier((value, *others))[0]


def masks(place, count):
    rows = lax.broadcasted_iota(jnp.int32, (count, place.shape[1]), 0)
    return rows == place[0:1, :], rows == place[1:2, :]


def slots_of(chosen, quota, count):
    tokens = chosen.shape[1]
    first, second = masks(chosen, count)
    first, second = jnp.where(first, 1.0, 0.0), jnp.where(second, 1.0, 0.0)
    row = lax.broadcasted_iota(jnp.int32, (tokens, tokens), 0)
    column = lax.broadcasted_iota(jnp.int32, (tokens, tokens), 1)
    earlier = jnp.where(row < column, 1.0, 0.0).astype(bf16)
    before = jnp.dot((first + second).astype(bf16), earlier, preferred_element_type=f32)
    slots = []
    for at, (mask, ranks) in enumerate(((first, before), (second, before + first))):
        ids = chosen[at : at + 1, :]
        rank = jnp.sum(mask * ranks, axis=0, keepdims=True).astype(jnp.int32)
        limit = jnp.zeros_like(ids)
        for expert in range(count):
            limit = jnp.where(ids == expert, quota[0, expert], limit)
        slots.append(jnp.where(rank < limit, ids * CAP + rank, -1))
    return slots


def dispatch_kernel(has_grad, quota, chosen_ref, weight_ref, scaling_ref, values_ref, *refs):
    grad_ref, (out, place_ref, inverse_ref) = refs[0], refs[-3:]
    count, _, tile = out.shape
    step = pl.program_id(0)

    @pl.when(step == 0)
    def _():
        values = values_ref[...].astype(f32)
        inverse_ref[...] = lax.rsqrt(jnp.mean(values * values, axis=1, keepdims=True) + EPSILON)
        first, second = slots_of(chosen_ref[...], quota, count)
        place_ref[0:1, :] = first
        place_ref[1:2, :] = second

    first, second = masks(place_ref[...], count * CAP)
    chosen = jnp.where(first | second, 1.0, 0.0).astype(bf16)
    values = values_ref[:, pl.ds(pl.multiple_of(step * tile, tile), tile)].astype(f32)
    normed = (values * inverse_ref[...] * scaling_ref[...]).astype(bf16)
    rows = jnp.dot(chosen, normed, preferred_element_type=f32)
    out[:, :CAP, :] = rows.astype(bf16).reshape(count, CAP, tile)
    if has_grad:
        weight = weight_ref[...]
        scale = jnp.where(first, weight[0:1, :], 0.0) + jnp.where(second, weight[1:2, :], 0.0)
        rows = jnp.dot(chosen, grad_ref[...], preferred_element_type=f32)
        rows = rows * jnp.sum(scale, axis=1, keepdims=True)
        out[:, CAP:, :] = rows.astype(bf16).reshape(count, CAP, tile)


def dispatch(quota, chosen, weight, scaling, values, grad=None):
    count, (tokens, width) = quota.shape[1], values.shape
    tile = 1024
    rows_each = CAP if grad is None else 2 * CAP
    column = pl.BlockSpec((tokens, tile), lambda i: (0, i))
    return pl.pallas_call(
        functools.partial(dispatch_kernel, grad is not None),
        grid=(width // tile,),
        in_specs=[
            pl.BlockSpec(memory_space=pltpu.SMEM),
            whole(chosen.shape),
            whole(weight.shape),
            pl.BlockSpec((1, tile), lambda i: (0, i)),
            whole(values.shape),
        ]
        + [column] * (grad is not None),
        out_specs=[
            pl.BlockSpec((count, rows_each, tile), lambda i: (0, 0, i)),
            whole(chosen.shape),
            whole((tokens, 1)),
        ],
        out_shape=[
            jax.ShapeDtypeStruct((count, rows_each, width), bf16),
            jax.ShapeDtypeStruct(chosen.shape, jnp.int32),
            jax.ShapeDtypeStruct((tokens, 1), f32),
        ],
        compiler_params=params(1),
        cost_estimate=cost(2 * count * rows_each * tokens * width, 2 * (count * rows_each + 2 * tokens) * width),
    )(quota, chosen, weight, scaling, values, *([] if grad is None else [grad]))


CHUNK = 256


def load(source, start, rows, semaphore):
    copy = pltpu.make_async_copy(source.at[:, pl.ds(start, CAP), :], rows, semaphore)
    copy.start()
    copy.wait()


def chunk_of(rows, at):
    blocks = CHUNK // CAP
    return rows[pl.ds(at * blocks, blocks)].reshape(CHUNK, rows.shape[2])


def forward_kernel(tiles, source, gate_w, up_w, down_w, out, rows, hidden, semaphore):
    step = pl.program_id(0)

    @pl.when(step == 0)
    def _():
        load(source, 0, rows, semaphore)

    for index in range(tiles):

        @pl.when(step == index)
        def _():
            @pl.loop(0, hidden.shape[0] // CHUNK)
            def _(at):
                span = pl.ds(pl.multiple_of(at * CHUNK, CHUNK), CHUNK)
                values = chunk_of(rows, at)
                gate = jnp.dot(values, gate_w[...], preferred_element_type=f32)
                up = jnp.dot(values, up_w[...], preferred_element_type=f32)
                size = gate_w.shape[1]
                value = gate / (1.0 + jnp.exp(-gate)) * up
                hidden[span, index * size : (index + 1) * size] = value.astype(bf16)

    @pl.when(step >= tiles)
    def _():
        out[...] = jnp.dot(hidden[...], down_w[...], preferred_element_type=f32).astype(bf16)


def expert_forward(source, gate_w, up_w, down_w):
    width, hid = gate_w.shape
    total = source.shape[0] * CAP
    tile, out_tile = 256, 1024
    tiles, out_tiles = hid // tile, width // out_tile
    project = pl.BlockSpec((width, tile), lambda i: (0, jnp.minimum(i, tiles - 1)))
    late = lambda i: (0, jnp.maximum(i - tiles, 0))
    return pl.pallas_call(
        functools.partial(forward_kernel, tiles),
        grid=(tiles + out_tiles,),
        in_specs=[ANY, project, project, pl.BlockSpec((hid, out_tile), late)],
        out_specs=pl.BlockSpec((total, out_tile), late),
        out_shape=jax.ShapeDtypeStruct((total, width), bf16),
        scratch_shapes=[
            pltpu.VMEM((source.shape[0], CAP, width), bf16),
            pltpu.VMEM((total, hid), bf16),
            pltpu.SemaphoreType.DMA,
        ],
        compiler_params=params(1),
        cost_estimate=cost(6 * total * width * hid, 6 * width * hid + 4 * total * width),
    )(source, gate_w, up_w, down_w)


def hidden_grad_kernel(source, down_w, out, rows, semaphore):
    @pl.when(pl.program_id(0) == 0)
    def _():
        load(source, CAP, rows, semaphore)

    @pl.loop(0, out.shape[0] // CHUNK)
    def _(at):
        span = pl.ds(pl.multiple_of(at * CHUNK, CHUNK), CHUNK)
        out[span, :] = lax.dot_general(
            chunk_of(rows, at), down_w[...], (((1,), (1,)), ((), ())), preferred_element_type=f32
        )


def expert_hidden_grad(source, down_w):
    hid, width = down_w.shape
    total = source.shape[0] * CAP
    tile = 256
    return pl.pallas_call(
        hidden_grad_kernel,
        grid=(hid // tile,),
        in_specs=[ANY, pl.BlockSpec((tile, width), lambda i: (i, 0))],
        out_specs=pl.BlockSpec((total, tile), lambda i: (0, i)),
        out_shape=jax.ShapeDtypeStruct((total, hid), f32),
        scratch_shapes=[pltpu.VMEM((source.shape[0], CAP, width), bf16), pltpu.SemaphoreType.DMA],
        compiler_params=params(1),
        cost_estimate=cost(2 * total * width * hid, 2 * width * hid + 2 * total * width),
    )(source, down_w)


def gate_grads_kernel(source, gate_w, up_w, hidden_ref, gate_out, up_out, rows, semaphore):
    @pl.when(pl.program_id(0) == 0)
    def _():
        load(source, 0, rows, semaphore)

    @pl.loop(0, gate_out.shape[0] // CHUNK)
    def _(at):
        span = pl.ds(pl.multiple_of(at * CHUNK, CHUNK), CHUNK)
        values = chunk_of(rows, at)
        gate = jnp.dot(values, gate_w[...], preferred_element_type=f32)
        up = jnp.dot(values, up_w[...], preferred_element_type=f32)
        hidden_grad = hidden_ref[span, :]
        sig = 1.0 / (1.0 + jnp.exp(-gate))
        gate_out[span, :] = (hidden_grad * up * sig * (1.0 + gate * (1.0 - sig))).astype(bf16)
        up_out[span, :] = (hidden_grad * gate * sig).astype(bf16)


def expert_gate_grads(source, gate_w, up_w, hidden_grad):
    width, hid = gate_w.shape
    total = source.shape[0] * CAP
    tile = 256
    project = pl.BlockSpec((width, tile), lambda i: (0, i))
    column = pl.BlockSpec((total, tile), lambda i: (0, i))
    return pl.pallas_call(
        gate_grads_kernel,
        grid=(hid // tile,),
        in_specs=[ANY, project, project, column],
        out_specs=[column, column],
        out_shape=[jax.ShapeDtypeStruct((total, hid), bf16)] * 2,
        scratch_shapes=[pltpu.VMEM((source.shape[0], CAP, width), bf16), pltpu.SemaphoreType.DMA],
        compiler_params=params(1),
        cost_estimate=cost(4 * total * width * hid, 4 * width * hid + 2 * total * width + 8 * total * hid),
    )(source, gate_w, up_w, hidden_grad)


def entry_grads_kernel(gate_grad, up_grad, gate_w, up_w, out):
    contract = (((1,), (1,)), ((), ()))

    @pl.loop(0, gate_grad.shape[0] // CHUNK)
    def _(at):
        span = pl.ds(pl.multiple_of(at * CHUNK, CHUNK), CHUNK)
        rows = lax.dot_general(gate_grad[span, :], gate_w[...], contract, preferred_element_type=f32)
        rows = rows + lax.dot_general(up_grad[span, :], up_w[...], contract, preferred_element_type=f32)
        out[span, :] = rows.astype(bf16)


def expert_entry_grads(gate_grad, up_grad, gate_w, up_w, part, parts):
    total, hid = gate_grad.shape
    width = gate_w.shape[0] // parts
    tile = 512
    steps = width // tile
    weights = pl.BlockSpec((tile, hid), lambda i: (part * steps + i, 0))
    return pl.pallas_call(
        entry_grads_kernel,
        grid=(steps,),
        in_specs=[whole(gate_grad.shape), whole(up_grad.shape), weights, weights],
        out_specs=pl.BlockSpec((total, tile), lambda i: (0, i)),
        out_shape=jax.ShapeDtypeStruct((total, width), bf16),
        compiler_params=params(1),
        cost_estimate=cost(4 * total * width * hid, 4 * width * hid + 2 * total * width + 4 * total * hid),
    )(gate_grad, up_grad, gate_w, up_w)


def exchange(pieces):
    return lax.all_to_all(pieces, "expert", split_axis=0, concat_axis=0, tiled=True)


def from_slots(place, table):
    return lax.dot_general(place, table, (((0,), (0,)), ((), ())), preferred_element_type=f32)


def input_grads_kernel(place, inverse_ref, scaling_ref, values_ref, grad_ref, table, out, scaled):
    step, tile = pl.program_id(0), table.shape[1]
    span = pl.ds(pl.multiple_of(step * tile, tile), tile)
    sums = jnp.dot(place[...], table[...], preferred_element_type=f32)
    scaled[:, span] = scaling_ref[:, span] * sums

    @pl.when(step == pl.num_programs(0) - 1)
    def _():
        values, inverse = values_ref[...].astype(f32), inverse_ref[...]
        inner = jnp.mean(values * scaled[...], axis=1, keepdims=True)
        result = grad_ref[...].astype(f32) + inverse * scaled[...]
        out[...] = (result - values * (inverse * inverse * inverse * inner)).astype(bf16)


def input_grads(place, inverse, scaling, values, grad, table):
    tokens, width = values.shape
    tile = 1024
    return pl.pallas_call(
        input_grads_kernel,
        grid=(width // tile,),
        in_specs=[
            whole(place.shape),
            whole(inverse.shape),
            whole(scaling.shape),
            whole(values.shape),
            whole(grad.shape),
            pl.BlockSpec((table.shape[0], tile), lambda i: (0, i)),
        ],
        out_specs=whole((tokens, width)),
        out_shape=jax.ShapeDtypeStruct((tokens, width), bf16),
        scratch_shapes=[pltpu.VMEM((tokens, width), f32)],
        compiler_params=params(1),
        cost_estimate=cost(2 * tokens * table.size, 2 * table.size + 6 * tokens * width),
    )(place, inverse, scaling, values, grad, table)


def written_kernel(source, out):
    out[...] = source[...]


def written(rows):
    block = pl.BlockSpec((rows.shape[0] // 2, rows.shape[1]), lambda i: (i, 0))
    return pl.pallas_call(
        written_kernel,
        grid=(2,),
        in_specs=[block],
        out_specs=block,
        out_shape=jax.ShapeDtypeStruct(rows.shape, rows.dtype),
        compiler_params=params(1),
        cost_estimate=cost(0, 4 * rows.size),
    )(rows)


def on_device(
    onward_block_activation,
    reverse_stored_activation,
    reverse_result_derivative,
    onward_specialist_choices,
    reverse_specialist_choices,
    onward_mixing_coefficients,
    reverse_mixing_coefficients,
    quota_table,
    rescaling_factor_list,
    gating_projection_matrix,
    expansion_matrix,
    contraction_matrix,
):
    scaling = rescaling_factor_list
    gate_w = gating_projection_matrix[0, 0]
    up_w = expansion_matrix[0, 0]
    down_w = contraction_matrix[0, 0]
    count, width = quota_table.shape[1], gate_w.shape[0]
    input_f, input_b, grad_y = onward_block_activation[0], reverse_stored_activation[0], reverse_result_derivative[0]
    weight_f, weight_b = onward_mixing_coefficients[0].T, reverse_mixing_coefficients[0].T
    chosen_f, chosen_b = onward_specialist_choices[0].T, reverse_specialist_choices[0].T

    send_f, slots_f, _ = dispatch(quota_table, chosen_f, weight_f, scaling, input_f)
    rows_f = exchange(send_f)
    send_b, slots_b, inverse_b = dispatch(quota_table, chosen_b, weight_b, scaling, input_b, grad_y)
    rows_b = exchange(after(send_b, rows_f))

    out_f = expert_forward(rows_f, gate_w, up_w, down_w)
    table_f = exchange(after(out_f, rows_b).reshape(count, CAP, width)).reshape(count * CAP, width)
    hidden_grad = expert_hidden_grad(rows_b, down_w)
    gate_grad, up_grad = expert_gate_grads(rows_b, gate_w, up_w, hidden_grad)
    out_b = expert_entry_grads(gate_grad, up_grad, gate_w, up_w, 0, 1)
    table_b = exchange(after(out_b, table_f).reshape(count, CAP, width)).reshape(count * CAP, width)

    first, second = masks(slots_f, count * CAP)
    mixed = jnp.where(first, weight_f[0:1, :], 0.0) + jnp.where(second, weight_f[1:2, :], 0.0)
    high = mixed.astype(bf16)
    low = (mixed - high.astype(f32)).astype(bf16)
    fwd = input_f.astype(f32) + from_slots(high, table_f) + from_slots(low, table_f)
    fwd_next = passed_along(fwd.astype(bf16), "pipe", 1)

    slot = lax.broadcasted_iota(jnp.int32, (input_b.shape[0], count * CAP), 1)
    place = ((slot == slots_b[0][:, None]) | (slot == slots_b[1][:, None])).astype(bf16)
    grad = input_grads(after(place, table_f), inverse_b, scaling, input_b, grad_y, table_b)
    grad_next = passed_along(grad, "pipe", -1)
    return (written(fwd_next)[None], grad_next[None])


def solution(mesh):
    blocks = P("pipe", "expert", None)
    in_specs = (blocks,) * 7 + (P("pipe", None),) * 2 + (P("pipe", "expert", None, None),) * 3
    return jax.shard_map(
        on_device, mesh=mesh, in_specs=in_specs, out_specs=(blocks, blocks), check_vma=False
    )
```
